512 devices in a mesh: row: 32 (over z_hi, x, core), col: 16 (over y, z_lo).
Axes of the slice: x: 4, y: 8, z: 8 (z_hi: 4, z_lo: 2; z = z_hi * 2 + z_lo), core: 2. Of those that a mesh axis runs over, the one named last changes fastest.
Arguments:
- tokens: bfloat16 [65536, 1024], P('row', 'col'), may hold values from -6 to 6
- up_weight: bfloat16 [1024, 4096], P('row', 'col'), may hold values from -0.1875 to 0.1875
- hidden_grad: bfloat16 [65536, 4096], P('row', 'col'), may hold values from -6 to 6
Outputs:
- hidden: bfloat16 [65536, 4096], P('row', 'col')
- input_grad: bfloat16 [65536, 1024], P('row', 'col')
The draws below stay inside these ranges and needn't reach their ends.
All inputs are finite; a program needn't handle non-finite values.
Results may differ from the reference program's by a relative error of at most 0.017.
Values may be sent and summed in bfloat16 or wider, within the bound.
A program may use at most 64 MiB of HBM per device.

```python
import jax
import jax.numpy as jnp
from jax import lax

D = 1024
FF = 4096
TOKENS = 65536
HID_BLOCK = 256


def levels(own_key, dims, shards, least, high):
    def one(position, blocks):
        steps = jax.random.uniform(jax.random.fold_in(jax.random.fold_in(own_key, 6), position), (blocks,), jnp.float32, least / len(shards), high / len(shards))
        return jnp.repeat(jnp.exp(steps), dims[position] // blocks).reshape((-1,) + (1,) * (len(dims) - position - 1))

    factor_of = one(*shards[0])
    for cut in shards[1:]:
        factor_of = factor_of * one(*cut)
    return factor_of


def noise(own_key, shape, scale, reach, pieces=(), kind=jnp.bfloat16):
    entries = scale * jax.random.normal(own_key, shape, jnp.float32)
    if pieces:
        entries = entries * levels(own_key, shape, pieces, -0.22, 0.18)
    return jnp.clip(entries, -reach, reach).astype(kind)


def setup_inputs(seed: int = 0) -> dict:
    seeds = jax.random.split(jax.random.key(seed), 4)
    tokens = noise(seeds[0], (TOKENS, D), 1.0, 6.0, ((0, 32), (1, 16)))
    up_weight = noise(seeds[1], (D, FF), D ** -0.5, 0.1875, ((0, 32), (1, 16)))
    hidden_grad = noise(seeds[2], (TOKENS, FF), 1.0, 6.0, ((0, 32), (1, 16)))
    return {"tokens": tokens, "up_weight": up_weight, "hidden_grad": hidden_grad}


gelu_c = 0.7978845608028654
gelu_a = 0.044715


def gelu_value(v):
    inner = gelu_c * (v + gelu_a * v * v * v)
    return 0.5 * v * (1.0 + jnp.tanh(inner))


def gelu_slope(v):
    inner = gelu_c * (v + gelu_a * v * v * v)
    tval = jnp.tanh(inner)
    return 0.5 * (1.0 + tval) + 0.5 * v * (1.0 - tval * tval) * gelu_c * (1.0 + 3.0 * gelu_a * v * v)


def reference(tokens, up_weight, hidden_grad):
    def one_block(running_total, block_index):
        begin_col = (block_index * HID_BLOCK).astype(jnp.int32)
        weights_block = lax.dynamic_slice_in_dim(up_weight, begin_col, HID_BLOCK, 1)
        preact = jnp.dot(tokens, weights_block, preferred_element_type=jnp.float32)
        hidden_block = gelu_value(preact).astype(jnp.bfloat16)
        grads_block = lax.dynamic_slice_in_dim(hidden_grad, begin_col, HID_BLOCK, 1)
        pre_grad = (grads_block.astype(jnp.float32) * gelu_slope(preact)).astype(jnp.bfloat16)
        term = lax.dot_general(pre_grad, weights_block, (((1,), (1,)), ((), ())), preferred_element_type=jnp.float32).astype(jnp.bfloat16)
        term = lax.optimization_barrier(term)
        return running_total + term.astype(jnp.float32), hidden_block

    blocks = jnp.arange(FF // HID_BLOCK, dtype=jnp.int32)
    start_total = jnp.zeros((TOKENS, D), jnp.float32)
    input_grad, hidden_blocks = lax.scan(one_block, start_total, blocks)
    hidden = jnp.transpose(hidden_blocks, (1, 0, 2)).reshape(TOKENS, FF)
    return hidden, input_grad.astype(jnp.bfloat16)
```

```python
import jax
import jax.numpy as jnp
from jax import lax
from jax.experimental import pallas as pl
from jax.experimental.pallas import tpu as pltpu
from jax.sharding import PartitionSpec as P

gelu_c = 0.7978845608028654
gelu_a = 0.044715

NZH, NX, NY = 4, 4, 8
NZ = 2 * NZH
CHUNKS = 4
MESH = pl.DeviceIdType.MESH
UP, DOWN = 0, 1


def chain(way, k):
    return NY // 2 if (k % 2 == 0) == (way == UP) else NY // 2 - 1


def kernel(
    tok_in, w_in, grad_in, hid_out, ig_out,
    tok_t, tok, wb, grad, hid, pre, pg, part, rs, fin,
    load_sem, tx_send, tx_recv, wz_send, wz_recv, wx_send, wx_recv, wc_send, wc_recv,
    hg_send, hg_recv, ag_send, ag_recv, rs_send, rs_recv, ho_send, ho_recv, io_send, io_recv, store_sem,
):
    feats, half = tok_in.shape[0], tok_in.shape[1] // 2
    size = half // CHUNKS
    wide = 2 * feats
    r, c = lax.axis_index("row"), lax.axis_index("col")
    y, zl = lax.div(c, 2), lax.rem(c, 2)
    zh, x, core = lax.div(r, 2 * NX), lax.rem(lax.div(r, 2), NX), lax.rem(r, 2)
    zo = 1 - zl
    z = 2 * zh + zl
    mine = pl.multiple_of(zl * half, half)
    other = pl.multiple_of(zo * half, half)

    def at_y(step):
        return lax.rem(y + step + NY, NY)

    def z_device(step):
        there = lax.rem(z + step, NZ)
        return ((lax.div(there, 2) * NX + x) * 2 + core, 2 * y + lax.rem(there, 2))

    def x_device(step):
        return ((zh * NX + lax.rem(x + step, NX)) * 2 + core, c)

    ring = ((r, 2 * at_y(1) + zl), (r, 2 * at_y(-1) + zl))
    partner = (r, c + 1 - 2 * zl)
    sibling = (r + 1 - 2 * core, c)

    def remote(src, dst, send, recv, device):
        return pltpu.make_async_remote_copy(
            src_ref=src, dst_ref=dst, send_sem=send, recv_sem=recv, device_id=device, device_id_type=MESH
        )

    loads = [
        pltpu.make_async_copy(
            tok_in.at[:, pl.ds(mine, half)], tok_t.at[pl.ds(pl.multiple_of(zl * feats, feats), feats)], load_sem.at[0]
        ),
        pltpu.make_async_copy(w_in, wb.at[zl, zh, x, core], load_sem.at[1]),
        pltpu.make_async_copy(grad_in.at[pl.ds(mine, half)], grad.at[zl], load_sem.at[2]),
    ]
    for load in loads:
        load.start()

    barrier = pltpu.get_barrier_semaphore()
    peers = [z_device(d) for d in range(1, NZ)] + [x_device(d) for d in range(1, NX)] + [*ring, sibling]
    for peer in peers:
        pl.semaphore_signal(barrier, inc=1, device_id=peer, device_id_type=MESH)
    pl.semaphore_wait(barrier, len(peers))

    sent = []

    def start(copy):
        copy.start()
        sent.append(copy)
        return copy

    tx = []
    for k in range(CHUNKS):
        there = pl.ds(pl.multiple_of(other + k * size, size), size)
        tx.append(
            start(
                remote(
                    tok_in.at[:, there],
                    tok_t.at[pl.ds(pl.multiple_of(zl * feats, feats), feats), pl.ds(k * size, size)],
                    tx_send.at[k], tx_recv.at[k], partner,
                )
            )
        )
    wz = [
        start(remote(w_in, wb.at[zl, zh, x, core], wz_send.at[d - 1], wz_recv.at[d - 1], z_device(d)))
        for d in range(1, NZ)
    ]

    def ag_copy(way, k, s):
        shard = tok.at[at_y(1 - s if way == UP else s - 1), pl.ds(k * size, size)]
        return remote(shard, shard, ag_send.at[way, k, s - 1], ag_recv.at[way, k, s - 1], ring[way])

    ag = {}
    loads[0].wait()
    for k in range(CHUNKS):
        tx[k].wait_recv()
        tok[y, k * size : (k + 1) * size, :] = jnp.transpose(tok_t[:, k * size : (k + 1) * size])
        for way in (UP, DOWN):
            ag[way, k, 1] = start(ag_copy(way, k, 1))

    def ag_step(k, s):
        for way in (UP, DOWN):
            if s <= chain(way, k):
                ag[way, k, s].wait_recv()
            if s < chain(way, k):
                ag[way, k, s + 1] = start(ag_copy(way, k, s + 1))

    hg = []
    for k in range(CHUNKS):
        here = pl.ds(pl.multiple_of(other + k * size, size), size)
        hg.append(
            start(remote(grad_in.at[here], grad.at[zl, pl.ds(k * size, size)], hg_send.at[k], hg_recv.at[k], partner))
        )

    loads[1].wait()
    for copy in wz:
        copy.wait_recv()
    wx = [
        start(remote(wb.at[:, :, x, core], wb.at[:, :, x, core], wx_send.at[d - 1], wx_recv.at[d - 1], x_device(d)))
        for d in range(1, NX)
    ]

    def to_sibling(d):
        block = wb.at[:, :, lax.rem(x + NX - d, NX), core]
        return start(remote(block, block, wc_send.at[d], wc_recv.at[d], sibling))

    wc = [to_sibling(0)]
    for k in range(CHUNKS):
        ag_step(k, 1)
    for d in range(1, NX):
        wx[d - 1].wait_recv()
        wc.append(to_sibling(d))
    for s in range(2, NY // 2):
        for k in range(CHUNKS):
            ag_step(k, s)
    for copy in wc:
        copy.wait_recv()
    loads[2].wait()

    depth, units = NY * wide, w_in.shape[1]

    def compute(k):
        rows = pl.ds(k * size, size)
        left = jnp.concatenate([tok[j, rows, :] for j in range(NY)], axis=1)
        for b in range(2):
            pre[b] = jnp.dot(left, wb[b].reshape(depth, units), preferred_element_type=jnp.float32)

        @pl.loop(0, size // 16)
        def _(i):
            for b in range(2):
                v = pre[b, pl.ds(pl.multiple_of(i * 16, 16), 16), :]
                u = v * v
                t = jnp.tanh(v * (gelu_c + gelu_c * gelu_a * u))
                h = 0.5 + 0.5 * t
                slope = h + (0.5 * v) * (1.0 - t * t) * (gelu_c + 3.0 * gelu_c * gelu_a * u)
                at = pl.ds(pl.multiple_of(k * size + i * 16, 16), 16)
                hid[b, at, :] = (v * h).astype(jnp.bfloat16)
                pg[pl.ds(pl.multiple_of(i * 16, 16), 16), b * units : (b + 1) * units] = (
                    grad[b, at, :].astype(jnp.float32) * slope
                ).astype(jnp.bfloat16)

        weights = jnp.concatenate([wb[b].reshape(depth, units) for b in range(2)], axis=1)
        part[k] = lax.dot_general(
            weights, pg[...], (((1,), (1,)), ((), ())), preferred_element_type=jnp.float32
        ).astype(jnp.bfloat16)

    def rs_rows(way, k, s):
        far = chain(way, k) - s + 1
        return pl.ds(pl.multiple_of(at_y(far if way == UP else -far) * wide, wide), wide)

    def rs_copy(way, k, s):
        return remote(
            part.at[k, rs_rows(way, k, s)], rs.at[way, k, s - 1],
            rs_send.at[way, k, s - 1], rs_recv.at[way, k, s - 1], ring[way],
        )

    rsum, ho, io, stores = {}, [], [], []
    for k in range(CHUNKS):
        ag_step(k, NY // 2)
        hg[k].wait_recv()
        compute(k)
        for way in (UP, DOWN):
            rsum[way, k, 1] = start(rs_copy(way, k, 1))
        rows = pl.ds(pl.multiple_of(mine + k * size, size), size)
        ho.append(
            start(remote(hid.at[zo, pl.ds(k * size, size)], hid_out.at[rows], ho_send.at[k], ho_recv.at[k], partner))
        )
        stores.append(pltpu.make_async_copy(hid.at[zl, pl.ds(k * size, size)], hid_out.at[rows], store_sem.at[0, k]))
        stores[-1].start()

    for s in range(2, NY // 2 + 2):
        for k in range(CHUNKS):
            for way in (UP, DOWN):
                if s <= chain(way, k):
                    rsum[way, k, s - 1].wait_recv()
                    rows = rs_rows(way, k, s)
                    part[k, rows, :] = (
                        part[k, rows, :].astype(jnp.float32) + rs[way, k, s - 2].astype(jnp.float32)
                    ).astype(jnp.bfloat16)
                    rsum[way, k, s] = start(rs_copy(way, k, s))
            if s == NY // 2 + 1:
                total = part[k, pl.ds(pl.multiple_of(y * wide, wide), wide), :].astype(jnp.float32)
                for way in (UP, DOWN):
                    rsum[way, k, chain(way, k)].wait_recv()
                    total += rs[way, k, chain(way, k) - 1].astype(jnp.float32)
                fin[k] = total.astype(jnp.bfloat16)
                columns = pl.ds(pl.multiple_of(mine + k * size, size), size)
                own = fin.at[k, pl.ds(pl.multiple_of(zl * feats, feats), feats)]
                theirs = fin.at[k, pl.ds(pl.multiple_of(zo * feats, feats), feats)]
                io.append(start(remote(theirs, ig_out.at[:, columns], io_send.at[k], io_recv.at[k], partner)))
                stores.append(pltpu.make_async_copy(own, ig_out.at[:, columns], store_sem.at[1, k]))
                stores[-1].start()

    for copy in ho + io:
        copy.wait_recv()
    for copy in sent:
        copy.wait_send()
    for copy in stores:
        copy.wait()


def per_device(tokens, up_weight, hidden_grad):
    rows, feats = tokens.shape
    half = rows // 2
    size = half // CHUNKS
    wide = 2 * feats
    units = up_weight.shape[1]
    depth = NY * wide
    bf16, f32 = jnp.bfloat16, jnp.float32
    dma = pltpu.SemaphoreType.DMA
    hops = NY // 2
    flops = 2 * 2 * half * depth * 2 * units
    hidden, ig = pl.pallas_call(
        kernel,
        out_shape=(
            jax.ShapeDtypeStruct((rows, units), bf16),
            jax.ShapeDtypeStruct((feats, rows), bf16),
        ),
        in_specs=[pl.BlockSpec(memory_space=pl.ANY)] * 3,
        out_specs=[pl.BlockSpec(memory_space=pl.ANY)] * 2,
        scratch_shapes=[
            pltpu.VMEM((wide, half), bf16),
            pltpu.VMEM((NY, half, wide), bf16),
            pltpu.VMEM((2, NZH, NX, 2, up_weight.shape[0], units), bf16),
            pltpu.VMEM((2, half, units), bf16),
            pltpu.VMEM((2, half, units), bf16),
            pltpu.VMEM((2, size, units), f32),
            pltpu.VMEM((size, 2 * units), bf16),
            pltpu.VMEM((CHUNKS, depth, size), bf16),
            pltpu.VMEM((2, CHUNKS, hops, wide, size), bf16),
            pltpu.VMEM((CHUNKS, wide, size), bf16),
            dma((3,)),
            dma((CHUNKS,)), dma((CHUNKS,)),
            dma((NZ - 1,)), dma((NZ - 1,)),
            dma((NX - 1,)), dma((NX - 1,)),
            dma((NX,)), dma((NX,)),
            dma((CHUNKS,)), dma((CHUNKS,)),
            dma((2, CHUNKS, hops)), dma((2, CHUNKS, hops)),
            dma((2, CHUNKS, hops)), dma((2, CHUNKS, hops)),
            dma((CHUNKS,)), dma((CHUNKS,)),
            dma((CHUNKS,)), dma((CHUNKS,)),
            dma((2, CHUNKS)),
        ],
        compiler_params=pltpu.CompilerParams(
            collective_id=0, has_side_effects=True, vmem_limit_bytes=48 * 1024 * 1024
        ),
        cost_estimate=pl.CostEstimate(flops=flops, bytes_accessed=6 * rows * units, transcendentals=rows * units),
    )(jnp.transpose(tokens), up_weight, hidden_grad)
    return hidden, jnp.transpose(ig)


def solution(mesh):
    in_specs = (P("row", "col"), P("row", "col"), P("row", "col"))
    out_specs = (P("row", "col"), P("row", "col"))
    return jax.shard_map(
        per_device, mesh=mesh, in_specs=in_specs, out_specs=out_specs, check_vma=False
    )
```

```python
import functools

import jax
import jax.numpy as jnp
from jax import lax
from jax.experimental import pallas as pl
from jax.experimental.pallas import tpu as pltpu
from jax.sharding import PartitionSpec as P

gelu_c = 0.7978845608028654
gelu_a = 0.044715

NZH, NX, NY = 4, 4, 8
NZ = 2 * NZH
CHUNKS, GROUP, EARLY = 8, 4, 4
HOPS = NY // 2
MESH = pl.DeviceIdType.MESH
UP, DOWN = 0, 1


def chain(way, k):
    return HOPS if (k % 2 == 0) == (way == UP) else HOPS - 1


def kernel(
    tok_in, w_in, grad_in, hid_out, ig_out,
    tok, wb, grad, hid, pre, pg, part, rs, fin,
    here, load_sem, tok_sem, tx_send, tx_recv, wz_send, wz_recv, wx_send, wx_recv, wc_send, wc_recv,
    hg_send, hg_recv, own_send, own_recv, ag_send, ag_recv, rs_send, rs_recv, ho_send, ho_recv, io_send, io_recv,
    store_sem,
):
    feats, half = tok_in.shape[0], tok_in.shape[1] // 2
    size = half // CHUNKS
    wide = 2 * feats
    depth, units = NY * wide, w_in.shape[1]
    r, c = lax.axis_index("row"), lax.axis_index("col")
    y, zl = lax.div(c, 2), lax.rem(c, 2)
    zh, x, core = lax.div(r, 2 * NX), lax.rem(lax.div(r, 2), NX), lax.rem(r, 2)
    zo = 1 - zl
    z = 2 * zh + zl
    mine, other = zl * half, zo * half
    own_rows = pl.ds(pl.multiple_of(zl * feats, feats), feats)
    their_rows = pl.ds(pl.multiple_of(zo * feats, feats), feats)

    def chunk(start, k, n=1):
        return pl.ds(pl.multiple_of(start + k * size, size), n * size)

    def at_y(step):
        return lax.rem(y + step + NY, NY)

    def z_device(step):
        there = lax.rem(z + step, NZ)
        return ((lax.div(there, 2) * NX + x) * 2 + core, 2 * y + lax.rem(there, 2))

    def x_device(step):
        return ((zh * NX + lax.rem(x + step, NX)) * 2 + core, c)

    ring = ((r, 2 * at_y(1) + zl), (r, 2 * at_y(-1) + zl))
    partner = (r, c + 1 - 2 * zl)
    sibling = (r + 1 - 2 * core, c)

    def remote(src, dst, send, recv, device):
        return pltpu.make_async_remote_copy(
            src_ref=src, dst_ref=dst, send_sem=send, recv_sem=recv, device_id=device, device_id_type=MESH
        )

    barrier = pltpu.get_barrier_semaphore()

    def signal(semaphore, device):
        pl.semaphore_signal(semaphore, inc=1, device_id=device, device_id_type=MESH)

    for device in (*ring, partner):
        signal(barrier, device)
    for d in range(1, NZ):
        pl.when(lax.div(lax.rem(z + d, NZ), 2) > zh)(functools.partial(signal, barrier, z_device(d)))
    for d in range(1, NX):
        pl.when(lax.rem(x + d, NX) < x)(functools.partial(signal, barrier, x_device(d)))
    pl.when(core == 1)(functools.partial(signal, barrier, sibling))

    def load_tokens(k):
        return pltpu.make_async_copy(tok_in.at[:, chunk(mine, k)], tok.at[k, y, own_rows], tok_sem.at[k])

    load_weights = pltpu.make_async_copy(w_in, wb.at[zl, zh, x, core], load_sem.at[0])
    load_grad = pltpu.make_async_copy(grad_in.at[chunk(mine, 0, CHUNKS)], grad.at[zl], load_sem.at[1])
    for k in range(CHUNKS):
        load_tokens(k).start()
    load_grad.start()

    load_weights.start()
    pl.semaphore_wait(barrier, 3 + 2 * zh + (NX - 1 - x) + (1 - core))
    for d in range(1, NZ):
        pl.when(lax.div(lax.rem(z + d, NZ), 2) < zh)(functools.partial(signal, here.at[0], z_device(d)))
    for d in range(1, NX):
        pl.when(lax.rem(x + d, NX) > x)(functools.partial(signal, here.at[1], x_device(d)))
    pl.when(core == 0)(functools.partial(signal, here.at[2], sibling))

    def wz_copy(d):
        return remote(w_in, wb.at[zl, zh, x, core], wz_send.at[d - 1], wz_recv.at[d - 1], z_device(d))

    def wx_copy(d):
        block = wb.at[:, :, x, core]
        return remote(block, block, wx_send.at[d - 1], wx_recv.at[d - 1], x_device(d))

    def wc_copy(d):
        block = wb.at[:, :, lax.rem(x + NX - d, NX), core]
        return remote(block, block, wc_send.at[d], wc_recv.at[d], sibling)

    def weights_z_known():
        for d in range(1, NZ):
            @pl.when(lax.div(lax.rem(z + d, NZ), 2) <= zh)
            def _():
                wz_copy(d).start()

    def weights_z():
        pl.when(zh < NZH - 1)(lambda: pl.semaphore_wait(here.at[0], NZ - 2 - 2 * zh))
        for d in range(1, NZ):
            @pl.when(lax.div(lax.rem(z + d, NZ), 2) > zh)
            def _():
                wz_copy(d).start()

    def weights_x():
        load_weights.wait()
        for d in range(1, NZ):
            wz_copy(d).wait_recv()
        pl.when(x > 0)(lambda: pl.semaphore_wait(here.at[1], x))
        for d in range(1, NX):
            wx_copy(d).start()
        pl.when(core == 1)(lambda: pl.semaphore_wait(here.at[2], 1))
        wc_copy(0).start()

    def weights_core():
        for d in range(1, NX):
            wx_copy(d).wait_recv()
            wc_copy(d).start()

    def weights_here():
        for d in range(NX):
            wc_copy(d).wait_recv()

    def weights_end():
        for d in range(1, NZ):
            wz_copy(d).wait_send()
        for d in range(1, NX):
            wx_copy(d).wait_send()
        for d in range(NX):
            wc_copy(d).wait_send()

    sent = []

    def start(copy):
        copy.start()
        sent.append(copy)
        return copy

    ag, own = {}, {}

    def ag_start(way, k, s):
        shard = tok.at[k, at_y(1 - s if way == UP else s - 1)]
        if s == 1 and k < EARLY:
            shard = shard.at[their_rows]
        ag[way, k, s] = start(
            remote(shard, shard, ag_send.at[way, k, s - 1], ag_recv.at[way, k, s - 1], ring[way])
        )

    def ag_step(k, s):
        for way in (UP, DOWN):
            if s <= chain(way, k):
                ag[way, k, s].wait_recv()
                if s == 1 and k < EARLY:
                    own[way, k].wait_recv()
            if s < chain(way, k):
                ag_start(way, k, s + 1)

    tx = []
    for k in range(CHUNKS):
        tx.append(
            start(
                remote(tok_in.at[:, chunk(other, k)], tok.at[k, y, own_rows], tx_send.at[k], tx_recv.at[k], partner)
            )
        )
        if k < EARLY:
            for way in (UP, DOWN):
                own[way, k] = start(
                    remote(
                        tok_in.at[:, chunk(mine, k)], tok.at[k, y, own_rows],
                        own_send.at[way, k], own_recv.at[way, k], ring[way],
                    )
                )

    weights_z_known()
    for k in range(CHUNKS):
        if k >= EARLY:
            load_tokens(k).wait()
        tx[k].wait_recv()
        for way in (UP, DOWN):
            ag_start(way, k, 1)

    hg = []
    for g in range(CHUNKS // GROUP):
        hg.append(
            start(
                remote(
                    grad_in.at[chunk(other, g * GROUP, GROUP)], grad.at[zl, chunk(0, g * GROUP, GROUP)],
                    hg_send.at[g], hg_recv.at[g], partner,
                )
            )
        )

    def compute(k):
        left = jnp.transpose(tok[k].reshape(depth, size))
        for b in range(2):
            pre[b] = jnp.dot(left, wb[b].reshape(depth, units), preferred_element_type=jnp.float32)

        @pl.loop(0, size // 32)
        def _(i):
            for b in range(2):
                rows = pl.ds(pl.multiple_of(i * 32, 32), 32)
                at = pl.ds(pl.multiple_of(k * size + i * 32, 32), 32)
                v = pre[b, rows, :]
                u = v * v
                t = jnp.tanh(v * (gelu_c + gelu_c * gelu_a * u))
                h = 0.5 + 0.5 * t
                slope = h + (0.5 * v) * (1.0 - t * t) * (gelu_c + 3.0 * gelu_c * gelu_a * u)
                hid[b, at, :] = (v * h).astype(jnp.bfloat16)
                pg[rows, b * units : (b + 1) * units] = (grad[b, at, :].astype(jnp.float32) * slope).astype(jnp.bfloat16)

        weights = jnp.concatenate([wb[b].reshape(depth, units) for b in range(2)], axis=1)
        part[k] = lax.dot_general(
            weights, pg[...], (((1,), (1,)), ((), ())), preferred_element_type=jnp.float32
        ).astype(jnp.bfloat16)

    ho, io, stores = [], [], []

    def store(src, dst, sem):
        stores.append(pltpu.make_async_copy(src, dst, sem))
        stores[-1].start()

    def hidden_out(k):
        rows = chunk(mine, k)
        ho.append(start(remote(hid.at[zo, chunk(0, k)], hid_out.at[rows], ho_send.at[k], ho_recv.at[k], partner)))
        store(hid.at[zl, chunk(0, k)], hid_out.at[rows], store_sem.at[0, k])

    rsum = {}

    def rs_rows(way, k, s):
        far_by = chain(way, k) - s + 1
        return pl.ds(pl.multiple_of(at_y(far_by if way == UP else -far_by) * wide, wide), wide)

    def rs_start(k, s):
        for way in (UP, DOWN):
            if s > chain(way, k):
                continue
            rows = rs_rows(way, k, s)
            if s > 1:
                rsum[way, k, s - 1].wait_recv()
                part[k, rows, :] = (
                    part[k, rows, :].astype(jnp.float32) + rs[way, k, s - 2].astype(jnp.float32)
                ).astype(jnp.bfloat16)
            rsum[way, k, s] = start(
                remote(
                    part.at[k, rows], rs.at[way, k, s - 1],
                    rs_send.at[way, k, s - 1], rs_recv.at[way, k, s - 1], ring[way],
                )
            )

    def finish(k):
        total = part[k, pl.ds(pl.multiple_of(y * wide, wide), wide), :].astype(jnp.float32)
        for way in (UP, DOWN):
            rsum[way, k, chain(way, k)].wait_recv()
            total += rs[way, k, chain(way, k) - 1].astype(jnp.float32)
        fin[k] = total.astype(jnp.bfloat16)
        columns = chunk(mine, k)
        io.append(start(remote(fin.at[k, their_rows], ig_out.at[:, columns], io_send.at[k], io_recv.at[k], partner)))
        store(fin.at[k, own_rows], ig_out.at[:, columns], store_sem.at[1, k])

    for k in (0, 1, 2, 3):
        ag_step(k, 1)
    for k in (4, 5):
        ag_step(k, 1)
    weights_z()
    for k in (0, 1, 2, 3):
        ag_step(k, 2)
    for k in (6, 7):
        ag_step(k, 1)
    weights_x()
    for k in (0, 1, 2, 3):
        ag_step(k, 3)
    for k in (4, 5, 6, 7):
        ag_step(k, 2)
    weights_core()
    for k in (4, 5, 6, 7):
        ag_step(k, 3)
    weights_here()
    load_grad.wait()
    hg[0].wait_recv()
    for k in (0, 1, 2, 3):
        ag_step(k, 4)
        if k < EARLY:
            load_tokens(k).wait()
        compute(k)
        rs_start(k, 1)
        hidden_out(k)
    hg[1].wait_recv()
    for k in (4, 5, 6, 7):
        rs_start(k - 4, 2)
        ag_step(k, 4)
        compute(k)
        rs_start(k, 1)
        hidden_out(k)
    for k in (0, 1, 2, 3):
        rs_start(k, 3)
    for k in (4, 5, 6, 7):
        rs_start(k, 2)
    for k in (4, 5, 6, 7):
        rs_start(k, 3)
    for k in range(CHUNKS):
        rs_start(k, 4)
    for k in range(CHUNKS):
        finish(k)

    for copy in ho + io:
        copy.wait_recv()
    for copy in sent:
        copy.wait_send()
    weights_end()
    for copy in stores:
        copy.wait()


def per_device(tokens, up_weight, hidden_grad):
    rows, feats = tokens.shape
    half = rows // 2
    size = half // CHUNKS
    wide = 2 * feats
    units = up_weight.shape[1]
    depth = NY * wide
    bf16, f32 = jnp.bfloat16, jnp.float32

    def pair(*shape):
        return [pltpu.SemaphoreType.DMA(shape)] * 2

    flops = 2 * 2 * half * depth * 2 * units
    hidden, ig = pl.pallas_call(
        kernel,
        out_shape=(
            jax.ShapeDtypeStruct((rows, units), bf16),
            jax.ShapeDtypeStruct((feats, rows), bf16),
        ),
        in_specs=[pl.BlockSpec(memory_space=pltpu.HBM)] * 3,
        out_specs=[pl.BlockSpec(memory_space=pl.ANY)] * 2,
        scratch_shapes=[
            pltpu.VMEM((CHUNKS, NY, wide, size), bf16),
            pltpu.VMEM((2, NZH, NX, 2, up_weight.shape[0], units), bf16),
            pltpu.VMEM((2, half, units), bf16),
            pltpu.VMEM((2, half, units), bf16),
            pltpu.VMEM((2, size, units), f32),
            pltpu.VMEM((size, 2 * units), bf16),
            pltpu.VMEM((CHUNKS, depth, size), bf16),
            pltpu.VMEM((2, CHUNKS, HOPS, wide, size), bf16),
            pltpu.VMEM((CHUNKS, wide, size), bf16),
            pltpu.SemaphoreType.REGULAR((3,)),
            pltpu.SemaphoreType.DMA((2,)),
            pltpu.SemaphoreType.DMA((CHUNKS,)),
            *pair(CHUNKS),
            *pair(NZ - 1),
            *pair(NX - 1),
            *pair(NX),
            *pair(CHUNKS // GROUP),
            *pair(2, EARLY),
            *pair(2, CHUNKS, HOPS),
            *pair(2, CHUNKS, HOPS),
            *pair(CHUNKS),
            *pair(CHUNKS),
            pltpu.SemaphoreType.DMA((2, CHUNKS)),
        ],
        compiler_params=pltpu.CompilerParams(
            collective_id=0, has_side_effects=True, vmem_limit_bytes=60 * 1024 * 1024
        ),
        cost_estimate=pl.CostEstimate(flops=flops, bytes_accessed=6 * rows * units, transcendentals=rows * units),
    )(jnp.transpose(tokens), up_weight, hidden_grad)
    return hidden, jnp.transpose(ig)


def solution(mesh):
    in_specs = (P("row", "col"), P("row", "col"), P("row", "col"))
    out_specs = (P("row", "col"), P("row", "col"))
    return jax.shard_map(
        per_device, mesh=mesh, in_specs=in_specs, out_specs=out_specs, check_vma=False
    )
```

```python
import functools

import jax
import jax.numpy as jnp
from jax import lax
from jax.experimental import pallas as pl
from jax.experimental.pallas import tpu as pltpu
from jax.sharding import PartitionSpec as P

gelu_c = 0.7978845608028654
gelu_a = 0.044715

NZH, NX, NY = 4, 4, 8
NZ = 2 * NZH
CHUNKS, GROUP, EARLY = 8, 4, 4
PIECES = 4
HOPS = NY // 2
MESH = pl.DeviceIdType.MESH
UP, DOWN = 0, 1


def chain(way, k):
    return HOPS if (k % 2 == 0) == (way == UP) else HOPS - 1


def kernel(
    tok_in, w_in, grad_in, hid_out, ig_out,
    tok, wb, grad, hid, pre, pg, part, rs, fin,
    here, load_sem, tok_sem, tx_send, tx_recv, wz_send, wz_recv, wx_send, wx_recv, wc_send, wc_recv,
    hg_send, hg_recv, own_send, own_recv, ag_send, ag_recv, rs_send, rs_recv, ho_send, ho_recv, io_send, io_recv,
    store_sem,
):
    feats, half = tok_in.shape[0], tok_in.shape[1] // 2
    size = half // CHUNKS
    wide = 2 * feats
    depth, units = NY * wide, w_in.shape[1]
    r, c = lax.axis_index("row"), lax.axis_index("col")
    y, zl = lax.div(c, 2), lax.rem(c, 2)
    zh, x, core = lax.div(r, 2 * NX), lax.rem(lax.div(r, 2), NX), lax.rem(r, 2)
    zo = 1 - zl
    z = 2 * zh + zl
    mine, other = zl * half, zo * half
    own_rows = pl.ds(pl.multiple_of(zl * feats, feats), feats)
    their_rows = pl.ds(pl.multiple_of(zo * feats, feats), feats)

    def chunk(start, k, n=1):
        return pl.ds(pl.multiple_of(start + k * size, size), n * size)

    def at_y(step):
        return lax.rem(y + step + NY, NY)

    def z_device(step):
        there = lax.rem(z + step, NZ)
        return ((lax.div(there, 2) * NX + x) * 2 + core, 2 * y + lax.rem(there, 2))

    def x_device(step):
        return ((zh * NX + lax.rem(x + step, NX)) * 2 + core, c)

    ring = ((r, 2 * at_y(1) + zl), (r, 2 * at_y(-1) + zl))
    partner = (r, c + 1 - 2 * zl)
    sibling = (r + 1 - 2 * core, c)

    def remote(src, dst, send, recv, device):
        return pltpu.make_async_remote_copy(
            src_ref=src, dst_ref=dst, send_sem=send, recv_sem=recv, device_id=device, device_id_type=MESH
        )

    barrier = pltpu.get_barrier_semaphore()

    def signal(semaphore, device):
        pl.semaphore_signal(semaphore, inc=1, device_id=device, device_id_type=MESH)

    for device in (*ring, partner):
        signal(barrier, device)
    for d in range(1, NZ):
        pl.when(lax.div(lax.rem(z + d, NZ), 2) > zh)(functools.partial(signal, barrier, z_device(d)))
    for d in range(1, NX):
        pl.when(lax.rem(x + d, NX) < x)(functools.partial(signal, barrier, x_device(d)))
    pl.when(core == 1)(functools.partial(signal, barrier, sibling))

    def load_tokens(k):
        return pltpu.make_async_copy(tok_in.at[:, chunk(mine, k)], tok.at[k, y, own_rows], tok_sem.at[k])

    load_weights = pltpu.make_async_copy(w_in, wb.at[zl, zh, x, core], load_sem.at[0])
    load_grad = pltpu.make_async_copy(grad_in.at[chunk(mine, 0, CHUNKS)], grad.at[zl], load_sem.at[1])
    for k in range(CHUNKS):
        load_tokens(k).start()
    load_grad.start()

    load_weights.start()
    pl.semaphore_wait(barrier, 3 + 2 * zh + (NX - 1 - x) + (1 - core))
    for d in range(1, NZ):
        pl.when(lax.div(lax.rem(z + d, NZ), 2) < zh)(functools.partial(signal, here.at[0], z_device(d)))
    for d in range(1, NX):
        pl.when(lax.rem(x + d, NX) > x)(functools.partial(signal, here.at[1], x_device(d)))
    pl.when(core == 0)(functools.partial(signal, here.at[2], sibling))

    def wz_copy(d):
        return remote(w_in, wb.at[zl, zh, x, core], wz_send.at[d - 1], wz_recv.at[d - 1], z_device(d))

    def wx_copy(d):
        block = wb.at[:, :, x, core]
        return remote(block, block, wx_send.at[d - 1], wx_recv.at[d - 1], x_device(d))

    def wc_copy(d):
        block = wb.at[:, :, lax.rem(x + NX - d, NX), core]
        return remote(block, block, wc_send.at[d], wc_recv.at[d], sibling)

    def weights_z_known():
        for d in range(1, NZ):
            @pl.when(lax.div(lax.rem(z + d, NZ), 2) <= zh)
            def _():
                wz_copy(d).start()

    def weights_z():
        pl.when(zh < NZH - 1)(lambda: pl.semaphore_wait(here.at[0], NZ - 2 - 2 * zh))
        for d in range(1, NZ):
            @pl.when(lax.div(lax.rem(z + d, NZ), 2) > zh)
            def _():
                wz_copy(d).start()

    def weights_x():
        load_weights.wait()
        for d in range(1, NZ):
            wz_copy(d).wait_recv()
        pl.when(x > 0)(lambda: pl.semaphore_wait(here.at[1], x))
        for d in range(1, NX):
            wx_copy(d).start()
        pl.when(core == 1)(lambda: pl.semaphore_wait(here.at[2], 1))
        wc_copy(0).start()

    def weights_core():
        for d in range(1, NX):
            wx_copy(d).wait_recv()
            wc_copy(d).start()

    def weights_here():
        for d in range(NX):
            wc_copy(d).wait_recv()

    def weights_end():
        for d in range(1, NZ):
            wz_copy(d).wait_send()
        for d in range(1, NX):
            wx_copy(d).wait_send()
        for d in range(NX):
            wc_copy(d).wait_send()

    sent = []

    def start(copy):
        copy.start()
        sent.append(copy)
        return copy

    ag, own = {}, {}

    def ag_start(way, k, s):
        shard = tok.at[k, at_y(1 - s if way == UP else s - 1)]
        if s == 1 and k < EARLY:
            shard = shard.at[their_rows]
        ag[way, k, s] = start(
            remote(shard, shard, ag_send.at[way, k, s - 1], ag_recv.at[way, k, s - 1], ring[way])
        )

    def ag_step(k, s):
        for way in (UP, DOWN):
            if s <= chain(way, k):
                ag[way, k, s].wait_recv()
                if s == 1 and k < EARLY:
                    own[way, k].wait_recv()
            if s < chain(way, k):
                ag_start(way, k, s + 1)

    tx = []
    for k in range(CHUNKS):
        tx.append(
            start(
                remote(tok_in.at[:, chunk(other, k)], tok.at[k, y, own_rows], tx_send.at[k], tx_recv.at[k], partner)
            )
        )
        if k < EARLY:
            for way in (UP, DOWN):
                own[way, k] = start(
                    remote(
                        tok_in.at[:, chunk(mine, k)], tok.at[k, y, own_rows],
                        own_send.at[way, k], own_recv.at[way, k], ring[way],
                    )
                )

    weights_z_known()
    for k in range(CHUNKS):
        if k >= EARLY:
            load_tokens(k).wait()
        tx[k].wait_recv()
        for way in (UP, DOWN):
            ag_start(way, k, 1)

    hg = []
    for g in range(CHUNKS // GROUP):
        hg.append(
            start(
                remote(
                    grad_in.at[chunk(other, g * GROUP, GROUP)], grad.at[zl, chunk(0, g * GROUP, GROUP)],
                    hg_send.at[g], hg_recv.at[g], partner,
                )
            )
        )

    def compute(k):
        left = jnp.concatenate([jnp.transpose(tok[k + i].reshape(depth, size)) for i in range(2)], axis=0)
        for b in range(2):
            pre[b] = jnp.dot(left, wb[b].reshape(depth, units), preferred_element_type=jnp.float32)

        @pl.loop(0, 2 * size // 32)
        def _(i):
            for b in range(2):
                rows = pl.ds(pl.multiple_of(i * 32, 32), 32)
                at = pl.ds(pl.multiple_of(k * size + i * 32, 32), 32)
                v = pre[b, rows, :]
                u = v * v
                t = jnp.tanh(v * (gelu_c + gelu_c * gelu_a * u))
                h = 0.5 + 0.5 * t
                slope = h + (0.5 * v) * (1.0 - t * t) * (gelu_c + 3.0 * gelu_c * gelu_a * u)
                hid[b, at, :] = (v * h).astype(jnp.bfloat16)
                pg[rows, b * units : (b + 1) * units] = (grad[b, at, :].astype(jnp.float32) * slope).astype(jnp.bfloat16)

        weights = jnp.concatenate([wb[b].reshape(depth, units) for b in range(2)], axis=1)
        terms = lax.dot_general(
            weights, pg[...], (((1,), (1,)), ((), ())), preferred_element_type=jnp.float32
        ).astype(jnp.bfloat16)
        for i in range(2):
            part[k + i] = terms[:, i * size : (i + 1) * size]

    ho, io, stores = [], [], []

    def store(src, dst, sem):
        stores.append(pltpu.make_async_copy(src, dst, sem))
        stores[-1].start()

    def hidden_out(k):
        rows = chunk(mine, k)
        ho.append(start(remote(hid.at[zo, chunk(0, k)], hid_out.at[rows], ho_send.at[k], ho_recv.at[k], partner)))
        store(hid.at[zl, chunk(0, k)], hid_out.at[rows], store_sem.at[0, k])

    rsum = {}

    def rs_rows(way, k, s):
        far_by = chain(way, k) - s + 1
        return pl.ds(pl.multiple_of(at_y(far_by if way == UP else -far_by) * wide, wide), wide)

    def rs_start(k, s):
        for way in (UP, DOWN):
            if s > chain(way, k):
                continue
            rows = rs_rows(way, k, s)
            if s > 1:
                rsum[way, k, s - 1].wait_recv()
                part[k, rows, :] = (
                    part[k, rows, :].astype(jnp.float32) + rs[way, k, s - 2].astype(jnp.float32)
                ).astype(jnp.bfloat16)
            rsum[way, k, s] = start(
                remote(
                    part.at[k, rows], rs.at[way, k, s - 1],
                    rs_send.at[way, k, s - 1], rs_recv.at[way, k, s - 1], ring[way],
                )
            )

    def finish(k):
        total = part[k, pl.ds(pl.multiple_of(y * wide, wide), wide), :].astype(jnp.float32)
        for way in (UP, DOWN):
            rsum[way, k, chain(way, k)].wait_recv()
            total += rs[way, k, chain(way, k) - 1].astype(jnp.float32)
        fin[k] = total.astype(jnp.bfloat16)
        columns = chunk(mine, k)
        io.append(start(remote(fin.at[k, their_rows], ig_out.at[:, columns], io_send.at[k], io_recv.at[k], partner)))
        store(fin.at[k, own_rows], ig_out.at[:, columns], store_sem.at[1, k])

    for k in (0, 1, 2, 3):
        ag_step(k, 1)
    for k in (4, 5):
        ag_step(k, 1)
    weights_z()
    for k in (0, 1, 2, 3):
        ag_step(k, 2)
    for k in (6, 7):
        ag_step(k, 1)
    weights_x()
    for k in (0, 1, 2, 3):
        ag_step(k, 3)
    for k in (4, 5, 6, 7):
        ag_step(k, 2)
    weights_core()
    for k in (4, 5, 6, 7):
        ag_step(k, 3)
    for k in (0,):
        ag_step(k, 4)
    weights_here()
    load_grad.wait()
    hg[0].wait_recv()
    for k in (0, 2):
        for i in (k, k + 1):
            if i > 0:
                ag_step(i, 4)
            if i < EARLY:
                load_tokens(i).wait()
        compute(k)
        for i in (k, k + 1):
            rs_start(i, 1)
            hidden_out(i)
    hg[1].wait_recv()
    for k in (4, 6):
        for i in (k, k + 1):
            rs_start(i - 4, 2)
            ag_step(i, 4)
        compute(k)
        for i in (k, k + 1):
            rs_start(i, 1)
            hidden_out(i)
    for k in (0, 1, 2, 3):
        rs_start(k, 3)
    for k in (4, 5, 6, 7):
        rs_start(k, 2)
    for k in (4, 5, 6, 7):
        rs_start(k, 3)
    for k in range(CHUNKS):
        rs_start(k, 4)
    for k in range(CHUNKS):
        finish(k)

    for copy in ho + io:
        copy.wait_recv()
    for copy in sent:
        copy.wait_send()
    weights_end()
    for copy in stores:
        copy.wait()


def write(hid_in, ig_in, hid_out, ig_out, hid, ig, load_sem, store_sem):
    rows, columns = hid_in.shape[0] // PIECES, ig_in.shape[1]
    ways = []
    for i in range(PIECES):
        at = pl.ds(i * rows, rows)
        ways.append((hid_in.at[at], hid.at[at], hid_out.at[at], i))
    ways.append((ig_in, ig, ig_out, PIECES))
    loads = [pltpu.make_async_copy(a, b, load_sem.at[i]) for a, b, _, i in ways]
    stores = [pltpu.make_async_copy(b, c, store_sem.at[i]) for _, b, c, i in ways]
    for load in loads:
        load.start()
    for load, store in zip(loads, stores):
        load.wait()
        store.start()
    for store in stores:
        store.wait()


def per_device(tokens, up_weight, hidden_grad):
    rows, feats = tokens.shape
    half = rows // 2
    size = half // CHUNKS
    wide = 2 * feats
    units = up_weight.shape[1]
    depth = NY * wide
    bf16, f32 = jnp.bfloat16, jnp.float32

    def pair(*shape):
        return [pltpu.SemaphoreType.DMA(shape)] * 2

    flops = 2 * 2 * half * depth * 2 * units
    hidden, ig = pl.pallas_call(
        kernel,
        out_shape=(
            jax.ShapeDtypeStruct((rows, units), bf16),
            jax.ShapeDtypeStruct((feats, rows), bf16),
        ),
        in_specs=[pl.BlockSpec(memory_space=pltpu.HBM)] * 3,
        out_specs=[pl.BlockSpec(memory_space=pl.ANY)] * 2,
        scratch_shapes=[
            pltpu.VMEM((CHUNKS, NY, wide, size), bf16),
            pltpu.VMEM((2, NZH, NX, 2, up_weight.shape[0], units), bf16),
            pltpu.VMEM((2, half, units), bf16),
            pltpu.VMEM((2, half, units), bf16),
            pltpu.VMEM((2, 2 * size, units), f32),
            pltpu.VMEM((2 * size, 2 * units), bf16),
            pltpu.VMEM((CHUNKS, depth, size), bf16),
            pltpu.VMEM((2, CHUNKS, HOPS, wide, size), bf16),
            pltpu.VMEM((CHUNKS, wide, size), bf16),
            pltpu.SemaphoreType.REGULAR((3,)),
            pltpu.SemaphoreType.DMA((2,)),
            pltpu.SemaphoreType.DMA((CHUNKS,)),
            *pair(CHUNKS),
            *pair(NZ - 1),
            *pair(NX - 1),
            *pair(NX),
            *pair(CHUNKS // GROUP),
            *pair(2, EARLY),
            *pair(2, CHUNKS, HOPS),
            *pair(2, CHUNKS, HOPS),
            *pair(CHUNKS),
            *pair(CHUNKS),
            pltpu.SemaphoreType.DMA((2, CHUNKS)),
        ],
        compiler_params=pltpu.CompilerParams(
            collective_id=0, has_side_effects=True, vmem_limit_bytes=60 * 1024 * 1024
        ),
        cost_estimate=pl.CostEstimate(flops=flops, bytes_accessed=6 * rows * units, transcendentals=rows * units),
    )(jnp.transpose(tokens), up_weight, hidden_grad)
    hidden, ig = pl.pallas_call(
        write,
        out_shape=(jax.ShapeDtypeStruct(hidden.shape, bf16), jax.ShapeDtypeStruct(ig.shape, bf16)),
        in_specs=[pl.BlockSpec(memory_space=pl.ANY)] * 2,
        out_specs=[pl.BlockSpec(memory_space=pl.ANY)] * 2,
        scratch_shapes=[
            pltpu.VMEM(hidden.shape, bf16), pltpu.VMEM(ig.shape, bf16),
            *pair(PIECES + 1),
        ],
    )(hidden, ig)
    return hidden, jnp.transpose(ig)


def solution(mesh):
    in_specs = (P("row", "col"), P("row", "col"), P("row", "col"))
    out_specs = (P("row", "col"), P("row", "col"))
    return jax.shard_map(
        per_device, mesh=mesh, in_specs=in_specs, out_specs=out_specs, check_vma=False
    )
```
